128 devices in a mesh: gx: 32 (over x, y, z_lo), gy: 4 (over z_hi, core).
Axes of the slice: x: 4, y: 4, z: 4 (z_hi: 2, z_lo: 2; z = z_hi * 2 + z_lo), core: 2. Of those that a mesh axis runs over, the one named last changes fastest.
Arguments:
- permeability: float32 [32768, 1024], P('gx', 'gy'), may hold values from 0.01 to 100
- basis: float32 [256, 8, 256, 256], P('gx', 'gy'), may hold values from 0 to 1, as said below
- support: int32 [256, 8, 256, 256], P('gx', 'gy'), may hold values from 0 to 1, as said below
Outputs:
- smoothed: float32 [256, 8, 256, 256], P('gx', 'gy')
The draws below stay inside these ranges and needn't reach their ends.
Inputs may be any that keep to these rules, and one draw needn't show every extreme that they name: support is 1 exactly on a rectangle of the box that contains the block's own 128 x 128 cells in its middle and reaches 32 to 64 cells past them on each side, cut to the grid. basis is positive where support is 1 and 0 elsewhere.
All inputs are finite; a program needn't handle non-finite values.
Results may differ from the reference program's by a relative error of at most 0.0003.
Values sent between devices are 32-bit elements; how exact they have to be, the bound alone decides.
No kernel may reach another device: no remote copies, remote signals or barrier semaphores. Data moves between devices by JAX's collectives and lax.ppermute only.
A program may use at most 128 MiB of HBM per device.

```python
import math
import jax
import jax.numpy as jnp

B = 128
H = 64
ITERS = 2
NX = 32768
NY = 1024
NBX = 256
NBY = 8


def support_parts(key):
    sides = jax.random.randint(jax.random.fold_in(key, 11), (NBX, NBY, 4), H // 2, H + 1)
    offsets = jnp.arange(2 * B, dtype=jnp.int32)
    start_x = (jnp.arange(NBX, dtype=jnp.int32) * B - H)[:, None, None] + offsets[None, None, :]
    start_y = (jnp.arange(NBY, dtype=jnp.int32) * B - H)[None, :, None] + offsets[None, None, :]
    in_x = (offsets[None, None, :] >= H - sides[:, :, 0:1]) & (offsets[None, None, :] < H + B + sides[:, :, 1:2])
    in_x = in_x & (start_x >= 0) & (start_x < NX)
    in_y = (offsets[None, None, :] >= H - sides[:, :, 2:3]) & (offsets[None, None, :] < H + B + sides[:, :, 3:4])
    in_y = in_y & (start_y >= 0) & (start_y < NY)
    return (in_x[:, :, :, None] & in_y[:, :, None, :]).astype(jnp.int32)


def draw_support(key, part):
    return support_parts(key)


def draw_basis(key, part):
    inside = support_parts(key).astype(jnp.float32)
    shape = (NBX, NBY, 2 * B, 2 * B)
    values = jnp.exp(jax.random.uniform(jax.random.fold_in(key, 23), shape, jnp.float32, jnp.log(0.05), 0.0))
    return values * inside


def levels(own_key, extent, pieces, smallest, top_value):
    loudness = 1.0
    for position, shards_of in pieces:
        draws = jax.random.uniform(jax.random.fold_in(jax.random.fold_in(own_key, 6), position), (shards_of,), jnp.float32, smallest / len(pieces), top_value / len(pieces))
        loudness = loudness * jnp.repeat(jnp.exp(draws), extent[position] // shards_of).reshape((-1,) + (1,) * (len(extent) - 1 - position))
    return loudness


def setup_inputs(seed: int = 0) -> dict:
    streams_of = jax.random.split(jax.random.key(seed), 4)
    return {
        "permeability": jnp.clip(jnp.exp(math.log(100.0) - 9.2103404 * jax.random.uniform(streams_of[0], (NX, NY), jnp.float32) ** levels(streams_of[0], (NX, NY), ((0, 32), (1, 4)), -0.2, 0.2)), 0.01, 100.0),
        "basis": draw_basis(jax.random.fold_in(streams_of[3], 71), 0),
        "support": draw_support(jax.random.fold_in(streams_of[3], 71), 0),
    }


relaxation = 2.0 / 3.0


def to_boxes(extended, count_x, count_y, block):
    tiles = extended.reshape(count_x + 1, block, count_y + 1, block).transpose(0, 2, 1, 3)
    upper = jnp.concatenate([tiles[:-1, :-1], tiles[:-1, 1:]], axis=3)
    lower = jnp.concatenate([tiles[1:, :-1], tiles[1:, 1:]], axis=3)
    return jnp.concatenate([upper, lower], axis=2)


def from_boxes(boxes, block):
    count_x, count_y = boxes.shape[0], boxes.shape[1]
    none = (0, 0)
    tiles = jnp.pad(boxes[:, :, :block, :block], ((0, 1), (0, 1), none, none))
    tiles = tiles + jnp.pad(boxes[:, :, :block, block:], ((0, 1), (1, 0), none, none))
    tiles = tiles + jnp.pad(boxes[:, :, block:, :block], ((1, 0), (0, 1), none, none))
    tiles = tiles + jnp.pad(boxes[:, :, block:, block:], ((1, 0), (1, 0), none, none))
    return tiles.transpose(0, 2, 1, 3).reshape((count_x + 1) * block, (count_y + 1) * block)


def harmonic(left, right):
    summed = left + right
    inside = summed > 0
    return jnp.where(inside, 2.0 * left * right / jnp.where(inside, summed, 1.0), 0.0)


def couplings(padded):
    faces_x = harmonic(padded[:-1, 1:-1], padded[1:, 1:-1])
    faces_y = harmonic(padded[1:-1, :-1], padded[1:-1, 1:])
    east = faces_x[1:]
    west = faces_x[:-1]
    north = faces_y[:, 1:]
    south = faces_y[:, :-1]
    diagonal = east + west + north + south
    return east, west, north, south, jnp.where(diagonal > 0, diagonal, 1.0)


def smooth(basis, support, east, west, north, south, diagonal):
    none = (0, 0)
    from_east = jnp.pad(basis[:, :, 1:, :], (none, none, (0, 1), none))
    from_west = jnp.pad(basis[:, :, :-1, :], (none, none, (1, 0), none))
    from_north = jnp.pad(basis[:, :, :, 1:], (none, none, none, (0, 1)))
    from_south = jnp.pad(basis[:, :, :, :-1], (none, none, none, (1, 0)))
    coupled = east * from_east + west * from_west + north * from_north + south * from_south
    return jnp.where(support > 0, (1.0 - relaxation) * basis + relaxation * coupled / diagonal, 0.0)


def reference(permeability, basis, support):
    padded = jnp.pad(permeability, H + 1)
    weights = tuple(to_boxes(field, NBX, NBY, B) for field in couplings(padded))
    for step in range(ITERS):
        basis = smooth(basis, support, *weights)
        summed = from_boxes(basis, B)
        summed = jnp.where(summed > 0, summed, 1.0)
        basis = basis / to_boxes(summed, NBX, NBY, B)
    return basis
```

```python
import jax
import jax.numpy as jnp
from jax import lax
from jax.experimental import pallas as pl
from jax.experimental.pallas import tpu as pltpu
from jax.sharding import PartitionSpec as P


F32 = jnp.float32
TINY = 1.1754944e-38
ROWS = 1224
PROWS = 1184
XR = 744
YR = 2720
CR = 480
GUARDS = ((0, 16, 280, 544, 808, 1072, 1216), (0, 144, 408, 672, 936, 1200, 1216))
VMEM_LIMIT = 48 * 1024 * 1024
WEIGH_ROWS = 64
FIRST_ROWS = 64
SECOND_ROWS = 64


def box_row(i):
    return 24 + 264 * (i // 2) if i % 2 == 0 else 152 + 264 * ((i - 1) // 2)


def chunk_rows(k):
    even = 24 + 264 * (k // 2) + 128 * (k % 2)
    odd = 152 + 264 * ((k - 1) // 2) + 128 * ((k - 1) % 2)
    return even, odd


def lanes(rows):
    return lax.broadcasted_iota(jnp.int32, (rows, 128), 1)


def sides():
    sx = 1 - lax.rem(lax.axis_index("gx"), 2)
    sy = 1 - lax.rem(lax.axis_index("gy"), 2)
    return (sx, 1 - sx), (sy, 1 - sy)


def pack_windows(pieces, first):
    rows = pieces[0].shape[0]
    lane = lanes(rows)
    out = jnp.zeros((rows, 128), F32)
    for c, piece in enumerate(pieces):
        turned = pltpu.roll(piece, (4 * c - first) % 128, 1)
        out = jnp.where(lane // 4 == c, turned, out)
    return out


def joined(pv, r, n):
    return jnp.where(lanes(n) < 64, pv[1, r:r + n], pv[0, r:r + n])


def mover(sem):
    moves = []

    def move(src, dst):
        c = pltpu.make_async_copy(src, dst, sem.at[len(moves)])
        c.start()
        moves.append(c)

    return moves, move


def pack_x_kernel(perm, basis, sx_e, sx_o, pv, mid, xfringe, sem, sem_in):
    (xe, xo), _ = sides()
    loads, load = mover(sem_in)
    moves, move = mover(sem)
    for t in (0, 1):
        for h in (0, 1):
            load(perm.at[pl.ds(952 * t, 72), pl.ds(128 * h, 128)], pv.at[t, h])
        for q in (0, 1):
            load(basis.at[7 * t, q, pl.ds(120 * t, 136), pl.ds(128 * (1 - q), 128)], mid.at[t, q, pl.ds(0, 136)])
            load(basis.at[1 + 5 * t, q, pl.ds(248 * t, 8), pl.ds(128 * (1 - q), 128)], mid.at[t, q, pl.ds(136, 8)])
    for t, out in ((xo, sx_o), (xe, sx_e)):
        for j in (0, 1):
            for h in (0, 1):
                at = 144 * (2 * j + h)
                r0 = pl.multiple_of(120 * t, 8)
                r1 = pl.multiple_of(248 * t, 8)
                move(basis.at[7 * t, j, pl.ds(r0, 136), pl.ds(128 * h, 128)], out.at[pl.ds(at, 136)])
                move(basis.at[1 + 5 * t, j, pl.ds(r1, 8), pl.ds(128 * h, 128)], out.at[pl.ds(at + 136, 8)])
        for h in (0, 1):
            r2 = pl.multiple_of(952 * t, 8)
            move(perm.at[pl.ds(r2, 72), pl.ds(128 * h, 128)], out.at[pl.ds(576 + 72 * h, 72)])
    for c in loads:
        c.wait()
    for t in (0, 1):
        for q in (0, 1):
            pieces = [mid[t, q, 8 * c:8 * c + 8] for c in range(18)]
            xfringe[t, 8 * q:8 * q + 8] = pack_windows(pieces, 126)
        xfringe[t, 16:24] = pack_windows([joined(pv[t], 8 * c, 8) for c in range(9)], 62)
    for t, out in ((xo, sx_o), (xe, sx_e)):
        move(xfringe.at[t], out.at[pl.ds(720, 24)])
    for c in moves:
        c.wait()


def pack_y_kernel(perm, basis, after, sy_e, sy_o, pv, mid, fringe, strip, sem, sem_in):
    _, (ye, yo) = sides()
    loads, load = mover(sem_in)
    moves, move = mover(sem)
    for h in (0, 1):
        load(perm.at[:, pl.ds(128 * h, 128)], pv.at[h])
    for q in (0, 1):
        load(basis.at[:, q, :, pl.ds(128 * (1 - q), 128)], mid.at[q])
    for s, out in ((yo, sy_o), (ye, sy_e)):
        lane = pl.multiple_of(s * 128, 128)
        for i in range(8):
            move(basis.at[i, s, :, pl.ds(lane, 128)], out.at[pl.ds(256 * i, 256)])
    for c in loads:
        c.wait()
    lane = lanes(32)
    for p in (0, 1):
        for q in (0, 1):
            pieces = [mid[q, 2 * (c // 8) + p, 32 * (c % 8):32 * (c % 8) + 32] for c in range(32)]
            fringe[32 * (2 * p + q):32 * (2 * p + q) + 32] = pack_windows(pieces, 126)
    fringe[128:160] = pack_windows([joined(pv, 32 * c, 32) for c in range(32)], 62)
    for h in (0, 1):
        for r in range(0, 512, 32):
            low = pv[h, r:r + 32]
            high = pltpu.roll(pv[h, r + 512:r + 544], 64, 1)
            keep = lane >= 64 if h else lane < 64
            strip[h, r:r + 32] = jnp.where(keep, low, high)
    for s, out in ((yo, sy_o), (ye, sy_e)):
        move(fringe.at[pl.ds(0, 128)], out.at[pl.ds(2048, 128)])
        move(strip.at[s], out.at[pl.ds(2176, 512)])
        move(fringe.at[pl.ds(128, 32)], out.at[pl.ds(2688, 32)])
    for c in moves:
        c.wait()


def corner_kernel(rx_e, rx_o, sc_e, sc_o):
    _, (ye, yo) = sides()
    for s, out in ((yo, sc_o), (ye, sc_e)):
        for slot, rx in ((0, rx_e), (1, rx_o)):
            base = 240 * slot
            m = pl.multiple_of(432 * s, 8)
            k = pl.multiple_of(576 + 72 * s, 8)
            out[base:base + 144] = rx[pl.ds(m, 144)]
            out[base + 144:base + 168] = rx[720:744]
            out[base + 168:base + 240] = rx[pl.ds(k, 72)]


def recip(x):
    r = pl.reciprocal(x, approx=True)
    return r * (2.0 - x * r)


def harmonic(a, b):
    return 2.0 * a * b * recip(jnp.maximum(a + b, TINY))


def main_kernel(perm, basis, rx_e, rx_o, ry_e, ry_o, rc_e, rc_o, out,
                a, b, pe, fx, w, pv, ps, fp, xp, cf, cp, res, sem, sem_out):
    (xe, xo), (ye, yo) = sides()
    copies = []

    def load(src, dst):
        c = pltpu.make_async_copy(src, dst, sem.at[len(copies)])
        c.start()
        copies.append(c)

    for h in (0, 1):
        load(perm.at[:, pl.ds(128 * h, 128)], pv.at[h])
    for s, ry in ((ye, ry_e), (yo, ry_o)):
        load(ry.at[pl.ds(2176, 512)], ps.at[s])
        load(ry.at[pl.ds(2048, 128)], fp.at[s, pl.ds(0, 128)])
        load(ry.at[pl.ds(2688, 32)], fp.at[s, pl.ds(128, 32)])
    for t, rx in ((xe, rx_e), (xo, rx_o)):
        load(rx.at[pl.ds(576, 144)], xp.at[t])
    for s, rc in ((ye, rc_e), (yo, rc_o)):
        for slot, t in ((0, xe), (1, xo)):
            load(rc.at[pl.ds(240 * slot + 144, 24)], cf.at[s, t])
            load(rc.at[pl.ds(240 * slot + 168, 72)], cp.at[s, t])
    early = len(copies)
    for i in range(8):
        for j in (0, 1):
            for h in (0, 1):
                load(basis.at[i, j, :, pl.ds(128 * h, 128)], a.at[i % 2, j, j + h, pl.ds(box_row(i), 256)])
        for s, ry in ((ye, ry_e), (yo, ry_o)):
            load(ry.at[pl.ds(256 * i, 256)], a.at[i % 2, 1 - s, 2 * s, pl.ds(box_row(i), 256)])

    def place(src, at, t, q, blk):
        r0 = pl.multiple_of(8 + 1072 * t, 8)
        r1 = pl.multiple_of(8 + 1200 * t, 8)
        load(src.at[pl.ds(at, 136)], a.at[1 - t, q, blk, pl.ds(r0, 136)])
        load(src.at[pl.ds(at + 136, 8)], a.at[t, q, blk, pl.ds(r1, 8)])

    for t, rx in ((xe, rx_e), (xo, rx_o)):
        for j in (0, 1):
            for h in (0, 1):
                place(rx, 144 * (2 * j + h), t, j, j + h)
    for s, rc in ((ye, rc_e), (yo, rc_o)):
        for slot, t in ((0, xe), (1, xo)):
            place(rc, 240 * slot, t, 1 - s, 2 * s)

    zero = jnp.zeros((8, 128), F32)
    for p in (0, 1):
        for q in (0, 1):
            for k in range(4):
                for g in GUARDS[p]:
                    a[p, q, k, g:g + 8] = zero
                    b[p, q, k, g:g + 8] = zero
    for k in range(4):
        pe[k, 0:8] = zero
        pe[k, PROWS - 8:PROWS] = zero
        fx[k, 0:8] = zero

    for c in copies[:early]:
        c.wait()

    def from_left(n):
        return lanes(n) % 4 < 2

    half32, half8 = lanes(32) < 64, lanes(8) < 64

    def fill(at, n, half, left, own0, own1, right):
        u0 = pltpu.roll(own0, 64, 1)
        u1 = pltpu.roll(own1, 64, 1)
        pe[0, at:at + n] = jnp.where(half, left, u0)
        pe[1, at:at + n] = jnp.where(half, u0, u1)
        pe[2, at:at + n] = jnp.where(half, u1, right)

    for r in range(0, 1024, 32):
        left, right = ps[0, r % 512:r % 512 + 32], ps[1, r % 512:r % 512 + 32]
        if r < 512:
            left, right = pltpu.roll(left, 64, 1), pltpu.roll(right, 64, 1)
        fill(80 + r, 32, half32, left, pv[0, r:r + 32], pv[1, r:r + 32], right)
    for t in (0, 1):
        for c in range(9):
            r = 8 * c
            left, right = pltpu.roll(cp[0, t, r:r + 8], 64, 1), pltpu.roll(cp[1, t, r:r + 8], 64, 1)
            fill(8 + 1096 * t + r, 8, half8, left, xp[t, r:r + 8], xp[t, 72 + r:80 + r], right)
        both = jnp.where(from_left(8), cf[0, t, 16:24], cf[1, t, 16:24])
        for c in range(9):
            r = 8 + 1096 * t + 8 * c
            pe[3, r:r + 8] = pltpu.roll(both, (126 - 4 * c) % 128, 1)
        for q in (0, 1):
            both = jnp.where(from_left(8), cf[0, t, 8 * q:8 * q + 8], cf[1, t, 8 * q:8 * q + 8])
            for c in range(18):
                r = 8 + 1072 * t + 8 * c if c < 17 else 8 + 1200 * t
                a[1 - t if c < 17 else t, q, 3, r:r + 8] = pltpu.roll(both, (126 - 4 * c) % 128, 1)
    both = jnp.where(from_left(32), fp[0, 128:160], fp[1, 128:160])
    for c in range(32):
        pe[3, 80 + 32 * c:112 + 32 * c] = pltpu.roll(both, (126 - 4 * c) % 128, 1)
    for p in (0, 1):
        for q in (0, 1):
            n = 32 * (2 * p + q)
            both = jnp.where(from_left(32), fp[0, n:n + 32], fp[1, n:n + 32])
            for c in range(32):
                r = box_row(2 * (c // 8) + p) + 32 * (c % 8)
                a[p, q, 3, r:r + 32] = pltpu.roll(both, (126 - 4 * c) % 128, 1)

    def edges(n):
        lane = lanes(n)
        return lane == 0, lane == 127

    def weigh(r, n):
        first, last = edges(n)
        here = [pe[k, pl.ds(r, n)] for k in range(4)]
        fxs = []
        for k in range(4):
            f = harmonic(here[k], pe[k, pl.ds(r + 1, n)])
            fx[k, pl.ds(r, n)] = f
            fxs.append(f)
        ahead = [pltpu.roll(x, 127, 1) for x in here]
        fys = [harmonic(here[k], jnp.where(last, ahead[(k + 1) % 4], ahead[k])) for k in range(4)]
        behind = [pltpu.roll(x, 1, 1) for x in fys]
        for k in range(4):
            west = fx[k, pl.ds(r - 1, n)]
            south = jnp.where(first, behind[(k + 3) % 4], behind[k])
            total = fxs[k] + west + fys[k] + south
            inv = 2.0 * recip(jnp.maximum(total, TINY))
            w[0, k, pl.ds(r, n)] = fxs[k] * inv
            w[1, k, pl.ds(r, n)] = west * inv
            w[2, k, pl.ds(r, n)] = fys[k] * inv
            w[3, k, pl.ds(r, n)] = south * inv

    def weigh_step(g, carry):
        weigh(pl.multiple_of(24 + WEIGH_ROWS * g, 8), WEIGH_ROWS)
        return carry

    weigh(8, 16)
    lax.fori_loop(0, 1152 // WEIGH_ROWS, weigh_step, 0)
    for c in copies[early:]:
        c.wait()

    def smooth(src, p, q, off, n, ws, blocks):
        first, last = edges(n)
        pairs = ((0, 1), (2, 3)) if q == 0 else ((3, 0), (1, 2))
        got = {}
        for x, y in pairs:
            bx, by = src[p, q, x, pl.ds(off, n)], src[p, q, y, pl.ds(off, n)]
            rx, ry = pltpu.roll(bx, 1, 1), pltpu.roll(by, 1, 1)
            lx, ly = pltpu.roll(bx, 127, 1), pltpu.roll(by, 127, 1)
            near = {
                x: (bx, jnp.where(last, ly, lx), jnp.where(first, 0.0, rx)),
                y: (by, jnp.where(last, 0.0, ly), jnp.where(first, rx, ry)),
            }
            for k in (x, y):
                if k not in blocks:
                    continue
                c, north, south = near[k]
                we, ww, wn, wsouth = ws[k]
                s = c + wn * north + wsouth * south
                s = s + we * src[p, q, k, pl.ds(off + 1, n)] + ww * src[p, q, k, pl.ds(off - 1, n)]
                got[k] = jnp.where(c > 0, s, 0.0)
        return got

    def group(src, wrow, offs, n, blocks):
        ws = {k: [w[d, k, pl.ds(wrow, n)] for d in range(4)] for k in blocks}
        s = {(p, q): smooth(src, p, q, offs[p], n, ws, blocks) for p in (0, 1) for q in (0, 1)}
        done = {}
        for k in blocks:
            total = (s[0, 0][k] + s[0, 1][k]) + (s[1, 0][k] + s[1, 1][k])
            inv = recip(jnp.maximum(total, TINY))
            for p in (0, 1):
                for q in (0, 1):
                    done[p, q, k] = s[p, q][k] * inv
        return done

    def first_pass(wrow, offs, n):
        for (p, q, k), v in group(a, wrow, offs, n, (0, 1, 2, 3)).items():
            b[p, q, k, pl.ds(offs[p], n)] = v

    first_pass(8, (8, 8), 8)
    first_pass(1168, (1208, 1208), 8)
    for k in range(9):
        even, odd = chunk_rows(k)

        def step(g, carry, k=k, even=even, odd=odd):
            r = pl.multiple_of(FIRST_ROWS * g, 8)
            offs = (pl.multiple_of(even + r, 8), pl.multiple_of(odd + r, 8))
            first_pass(pl.multiple_of(16 + 128 * k + r, 8), offs, FIRST_ROWS)
            return carry

        lax.fori_loop(0, 128 // FIRST_ROWS, step, 0)

    stores = []
    for k in range(9):
        even, odd = chunk_rows(k)
        boxes = ((k // 2) * 2, ((k + 1) // 2) * 2 - 1)

        def step(g, carry, k=k, even=even, odd=odd, boxes=boxes):
            r = pl.multiple_of(SECOND_ROWS * g, 8)
            offs = (pl.multiple_of(even + r, 8), pl.multiple_of(odd + r, 8))
            done = group(b, pl.multiple_of(16 + 128 * k + r, 8), offs, SECOND_ROWS, (0, 1, 2))
            for p in (0, 1):
                i = boxes[p]
                if not 0 <= i < 8:
                    continue
                for j in (0, 1):
                    for h in (0, 1):
                        res[i, j, h, pl.ds(128 * (k - i) + r, SECOND_ROWS)] = done[p, j, j + h]
            return carry

        lax.fori_loop(0, 128 // SECOND_ROWS, step, 0)
        if k >= 1:
            for j in (0, 1):
                for h in (0, 1):
                    c = pltpu.make_async_copy(res.at[k - 1, j, h], out.at[k - 1, j, :, pl.ds(128 * h, 128)], sem_out.at[len(stores)])
                    c.start()
                    stores.append(c)
    for c in stores:
        c.wait()


def both_ways(pairs):
    return pairs + [(d, s) for s, d in pairs]


def swap(block, axis, parity):
    n = lax.axis_size(axis)
    return lax.ppermute(block, axis, both_ways([(i, i + 1) for i in range(parity, n - 1, 2)]))


def hbm(n):
    return [pl.BlockSpec(memory_space=pltpu.HBM)] * n


def bundle(rows):
    return jax.ShapeDtypeStruct((rows, 128), F32)


def local(permeability, basis, support):
    params = pltpu.CompilerParams(vmem_limit_bytes=VMEM_LIMIT)
    dma = pltpu.SemaphoreType.DMA
    sx_e, sx_o = pl.pallas_call(
        pack_x_kernel,
        out_shape=[bundle(XR), bundle(XR)],
        in_specs=hbm(2),
        out_specs=hbm(2),
        scratch_shapes=[
            pltpu.VMEM((2, 2, 72, 128), F32),
            pltpu.VMEM((2, 2, 144, 128), F32),
            pltpu.VMEM((2, 24, 128), F32),
            dma((22,)),
            dma((12,)),
        ],
        compiler_params=pltpu.CompilerParams(vmem_limit_bytes=16 * 1024 * 1024),
        name="pack_x",
    )(permeability, basis)
    rx_o = swap(sx_o, "gx", 1)
    rx_e = swap(sx_e, "gx", 0)
    sy_e, sy_o = pl.pallas_call(
        pack_y_kernel,
        out_shape=[bundle(YR), bundle(YR)],
        in_specs=hbm(3),
        out_specs=hbm(2),
        scratch_shapes=[
            pltpu.VMEM((2, 1024, 128), F32),
            pltpu.VMEM((2, 8, 256, 128), F32),
            pltpu.VMEM((160, 128), F32),
            pltpu.VMEM((2, 512, 128), F32),
            dma((22,)),
            dma((4,)),
        ],
        compiler_params=pltpu.CompilerParams(vmem_limit_bytes=16 * 1024 * 1024),
        name="pack_y",
    )(permeability, basis, sx_e)
    ry_o = swap(sy_o, "gy", 1)
    ry_e = swap(sy_e, "gy", 0)
    sc_e, sc_o = pl.pallas_call(
        corner_kernel,
        out_shape=[bundle(CR), bundle(CR)],
        in_specs=[pl.BlockSpec(memory_space=pltpu.VMEM)] * 2,
        out_specs=[pl.BlockSpec(memory_space=pltpu.VMEM)] * 2,
        compiler_params=pltpu.CompilerParams(vmem_limit_bytes=4 * 1024 * 1024),
        name="corner",
    )(rx_e, rx_o)
    rc_o = swap(sc_o, "gy", 1)
    rc_e = swap(sc_e, "gy", 0)
    return pl.pallas_call(
        main_kernel,
        out_shape=jax.ShapeDtypeStruct(basis.shape, F32),
        in_specs=hbm(8),
        out_specs=pl.BlockSpec(memory_space=pltpu.HBM),
        scratch_shapes=[
            pltpu.VMEM((2, 2, 4, ROWS, 128), F32),
            pltpu.VMEM((2, 2, 4, ROWS, 128), F32),
            pltpu.VMEM((4, PROWS, 128), F32),
            pltpu.VMEM((4, PROWS, 128), F32),
            pltpu.VMEM((4, 4, PROWS, 128), F32),
            pltpu.VMEM((2, 1024, 128), F32),
            pltpu.VMEM((2, 512, 128), F32),
            pltpu.VMEM((2, 160, 128), F32),
            pltpu.VMEM((2, 144, 128), F32),
            pltpu.VMEM((2, 2, 24, 128), F32),
            pltpu.VMEM((2, 2, 72, 128), F32),
            pltpu.VMEM((8, 2, 2, 256, 128), F32),
            dma((96,)),
            dma((32,)),
        ],
        compiler_params=params,
        name="smooth",
    )(permeability, basis, rx_e, rx_o, ry_e, ry_o, rc_e, rc_o)


def solution(mesh):
    placed = (P("gx", "gy"), P("gx", "gy", None, None), P("gx", "gy", None, None))
    return jax.shard_map(
        local, mesh=mesh, in_specs=placed, out_specs=P("gx", "gy", None, None), check_vma=False
    )
```

```python
import jax
import jax.numpy as jnp
from jax import lax
from jax.experimental import pallas as pl
from jax.experimental.pallas import tpu as pltpu
from jax.sharding import PartitionSpec as P


F32 = jnp.float32
TINY = 1.1754944e-38
ROWS = 1224
PROWS = 1184
XR = 744
YR = 2720
CR = 480
GUARDS = ((0, 16, 280, 544, 808, 1072, 1216), (0, 144, 408, 672, 936, 1200, 1216))
VMEM_LIMIT = 60 * 1024 * 1024
SUB = 8
PACK_LIMIT = 16 * 1024 * 1024
WEIGH_ROWS = 64
FIRST_ROWS = 128
SECOND_ROWS = 128


def box_row(i):
    return 24 + 264 * (i // 2) if i % 2 == 0 else 152 + 264 * ((i - 1) // 2)


def chunk_rows(k):
    even = 24 + 264 * (k // 2) + 128 * (k % 2)
    odd = 152 + 264 * ((k - 1) // 2) + 128 * ((k - 1) % 2)
    return even, odd


def lanes(rows):
    return lax.broadcasted_iota(jnp.int32, (rows, 128), 1)


def sides():
    sx = 1 - lax.rem(lax.axis_index("gx"), 2)
    sy = 1 - lax.rem(lax.axis_index("gy"), 2)
    return (sx, 1 - sx), (sy, 1 - sy)


def pack_windows(pieces, first):
    rows = pieces[0].shape[0]
    lane = lanes(rows)
    out = jnp.zeros((rows, 128), F32)
    for c, piece in enumerate(pieces):
        turned = pltpu.roll(piece, (4 * c - first) % 128, 1)
        out = jnp.where(lane // 4 == c, turned, out)
    return out


def joined(pv, r, n):
    return jnp.where(lanes(n) < 64, pv[1, r:r + n], pv[0, r:r + n])


def mover(sem):
    moves = []

    def move(src, dst):
        c = pltpu.make_async_copy(src, dst, sem.at[len(moves)])
        c.start()
        moves.append(c)

    return moves, move


def pack_x_kernel(perm, basis, sx_e, sx_o, pv, mid, xfringe, sem, sem_in):
    (xe, xo), _ = sides()
    loads, load = mover(sem_in)
    moves, move = mover(sem)
    for t in (0, 1):
        for h in (0, 1):
            load(perm.at[pl.ds(952 * t, 72), pl.ds(128 * h, 128)], pv.at[t, h])
        for q in (0, 1):
            load(basis.at[7 * t, q, pl.ds(120 * t, 136), pl.ds(128 * (1 - q), 128)], mid.at[t, q, pl.ds(0, 136)])
            load(basis.at[1 + 5 * t, q, pl.ds(248 * t, 8), pl.ds(128 * (1 - q), 128)], mid.at[t, q, pl.ds(136, 8)])
    for t, out in ((xo, sx_o), (xe, sx_e)):
        for j in (0, 1):
            for h in (0, 1):
                at = 144 * (2 * j + h)
                r0 = pl.multiple_of(120 * t, 8)
                r1 = pl.multiple_of(248 * t, 8)
                move(basis.at[7 * t, j, pl.ds(r0, 136), pl.ds(128 * h, 128)], out.at[pl.ds(at, 136)])
                move(basis.at[1 + 5 * t, j, pl.ds(r1, 8), pl.ds(128 * h, 128)], out.at[pl.ds(at + 136, 8)])
        for h in (0, 1):
            r2 = pl.multiple_of(952 * t, 8)
            move(perm.at[pl.ds(r2, 72), pl.ds(128 * h, 128)], out.at[pl.ds(576 + 72 * h, 72)])
    for c in loads:
        c.wait()
    for t in (0, 1):
        for q in (0, 1):
            pieces = [mid[t, q, 8 * c:8 * c + 8] for c in range(18)]
            xfringe[t, 8 * q:8 * q + 8] = pack_windows(pieces, 126)
        xfringe[t, 16:24] = pack_windows([joined(pv[t], 8 * c, 8) for c in range(9)], 62)
    for t, out in ((xo, sx_o), (xe, sx_e)):
        move(xfringe.at[t], out.at[pl.ds(720, 24)])
    for c in moves:
        c.wait()


def pack_y_kernel(perm, basis, after, sy_e, sy_o, pv, mid, fringe, strip, sem, sem_in):
    _, (ye, yo) = sides()
    loads, load = mover(sem_in)
    moves, move = mover(sem)
    for h in (0, 1):
        load(perm.at[:, pl.ds(128 * h, 128)], pv.at[h])
    for q in (0, 1):
        load(basis.at[:, q, :, pl.ds(128 * (1 - q), 128)], mid.at[q])
    for s, out in ((yo, sy_o), (ye, sy_e)):
        lane = pl.multiple_of(s * 128, 128)
        for i in range(8):
            move(basis.at[i, s, :, pl.ds(lane, 128)], out.at[pl.ds(256 * i, 256)])
    for c in loads:
        c.wait()
    lane = lanes(32)
    for p in (0, 1):
        for q in (0, 1):
            pieces = [mid[q, 2 * (c // 8) + p, 32 * (c % 8):32 * (c % 8) + 32] for c in range(32)]
            fringe[32 * (2 * p + q):32 * (2 * p + q) + 32] = pack_windows(pieces, 126)
    fringe[128:160] = pack_windows([joined(pv, 32 * c, 32) for c in range(32)], 62)
    for h in (0, 1):
        for r in range(0, 512, 32):
            low = pv[h, r:r + 32]
            high = pltpu.roll(pv[h, r + 512:r + 544], 64, 1)
            keep = lane >= 64 if h else lane < 64
            strip[h, r:r + 32] = jnp.where(keep, low, high)
    for s, out in ((yo, sy_o), (ye, sy_e)):
        move(fringe.at[pl.ds(0, 128)], out.at[pl.ds(2048, 128)])
        move(strip.at[s], out.at[pl.ds(2176, 512)])
        move(fringe.at[pl.ds(128, 32)], out.at[pl.ds(2688, 32)])
    for c in moves:
        c.wait()


def gate_kernel(y_e, y_o, after, out_e, out_o):
    pass


def corner_kernel(rx_e, rx_o, sc_e, sc_o):
    _, (ye, yo) = sides()
    for s, out in ((yo, sc_o), (ye, sc_e)):
        for slot, rx in ((0, rx_e), (1, rx_o)):
            base = 240 * slot
            m = pl.multiple_of(432 * s, 8)
            k = pl.multiple_of(576 + 72 * s, 8)
            out[base:base + 144] = rx[pl.ds(m, 144)]
            out[base + 144:base + 168] = rx[720:744]
            out[base + 168:base + 240] = rx[pl.ds(k, 72)]


def recip(x):
    r = pl.reciprocal(x, approx=True)
    return r * (2.0 - x * r)


def harmonic(a, b):
    return 2.0 * a * b * recip(jnp.maximum(a + b, TINY))


def main_kernel(perm, basis, rx_e, rx_o, ry_e, ry_o, rc_e, rc_o, out,
                a, b, pe, fx, w, pv, ps, fp, xp, cf, cp, res, sem, sem_out):
    (xe, xo), (ye, yo) = sides()
    copies = []

    def load(src, dst):
        c = pltpu.make_async_copy(src, dst, sem.at[len(copies)])
        c.start()
        copies.append(c)

    for h in (0, 1):
        load(perm.at[:, pl.ds(128 * h, 128)], pv.at[h])
    for s, ry in ((ye, ry_e), (yo, ry_o)):
        load(ry.at[pl.ds(2176, 512)], ps.at[s])
        load(ry.at[pl.ds(2048, 128)], fp.at[s, pl.ds(0, 128)])
        load(ry.at[pl.ds(2688, 32)], fp.at[s, pl.ds(128, 32)])
    for t, rx in ((xe, rx_e), (xo, rx_o)):
        load(rx.at[pl.ds(576, 144)], xp.at[t])
    for s, rc in ((ye, rc_e), (yo, rc_o)):
        for slot, t in ((0, xe), (1, xo)):
            load(rc.at[pl.ds(240 * slot + 144, 24)], cf.at[s, t])
            load(rc.at[pl.ds(240 * slot + 168, 72)], cp.at[s, t])
    early = len(copies)
    for i in range(8):
        for j in (0, 1):
            for h in (0, 1):
                load(basis.at[i, j, :, pl.ds(128 * h, 128)], a.at[i % 2, j, j + h, pl.ds(box_row(i), 256)])
        for s, ry in ((ye, ry_e), (yo, ry_o)):
            load(ry.at[pl.ds(256 * i, 256)], a.at[i % 2, 1 - s, 2 * s, pl.ds(box_row(i), 256)])

    def place(src, at, t, q, blk):
        r0 = pl.multiple_of(8 + 1072 * t, 8)
        r1 = pl.multiple_of(8 + 1200 * t, 8)
        load(src.at[pl.ds(at, 136)], a.at[1 - t, q, blk, pl.ds(r0, 136)])
        load(src.at[pl.ds(at + 136, 8)], a.at[t, q, blk, pl.ds(r1, 8)])

    for t, rx in ((xe, rx_e), (xo, rx_o)):
        for j in (0, 1):
            for h in (0, 1):
                place(rx, 144 * (2 * j + h), t, j, j + h)
    for s, rc in ((ye, rc_e), (yo, rc_o)):
        for slot, t in ((0, xe), (1, xo)):
            place(rc, 240 * slot, t, 1 - s, 2 * s)

    zero = jnp.zeros((8, 128), F32)
    for p in (0, 1):
        for q in (0, 1):
            for k in range(4):
                for g in GUARDS[p]:
                    a[p, q, k, g:g + 8] = zero
                    b[p, q, k, g:g + 8] = zero
    for k in range(4):
        pe[k, 0:8] = zero
        pe[k, PROWS - 8:PROWS] = zero
        fx[k, 0:8] = zero

    for c in copies[:early]:
        c.wait()

    def from_left(n):
        return lanes(n) % 4 < 2

    half32, half8 = lanes(32) < 64, lanes(8) < 64

    def fill(at, n, half, left, own0, own1, right):
        u0 = pltpu.roll(own0, 64, 1)
        u1 = pltpu.roll(own1, 64, 1)
        pe[0, at:at + n] = jnp.where(half, left, u0)
        pe[1, at:at + n] = jnp.where(half, u0, u1)
        pe[2, at:at + n] = jnp.where(half, u1, right)

    for r in range(0, 1024, 32):
        left, right = ps[0, r % 512:r % 512 + 32], ps[1, r % 512:r % 512 + 32]
        if r < 512:
            left, right = pltpu.roll(left, 64, 1), pltpu.roll(right, 64, 1)
        fill(80 + r, 32, half32, left, pv[0, r:r + 32], pv[1, r:r + 32], right)
    for t in (0, 1):
        for c in range(9):
            r = 8 * c
            left, right = pltpu.roll(cp[0, t, r:r + 8], 64, 1), pltpu.roll(cp[1, t, r:r + 8], 64, 1)
            fill(8 + 1096 * t + r, 8, half8, left, xp[t, r:r + 8], xp[t, 72 + r:80 + r], right)
        both = jnp.where(from_left(8), cf[0, t, 16:24], cf[1, t, 16:24])
        for c in range(9):
            r = 8 + 1096 * t + 8 * c
            pe[3, r:r + 8] = pltpu.roll(both, (126 - 4 * c) % 128, 1)
        for q in (0, 1):
            both = jnp.where(from_left(8), cf[0, t, 8 * q:8 * q + 8], cf[1, t, 8 * q:8 * q + 8])
            for c in range(18):
                r = 8 + 1072 * t + 8 * c if c < 17 else 8 + 1200 * t
                a[1 - t if c < 17 else t, q, 3, r:r + 8] = pltpu.roll(both, (126 - 4 * c) % 128, 1)
    both = jnp.where(from_left(32), fp[0, 128:160], fp[1, 128:160])
    for c in range(32):
        pe[3, 80 + 32 * c:112 + 32 * c] = pltpu.roll(both, (126 - 4 * c) % 128, 1)
    for p in (0, 1):
        for q in (0, 1):
            n = 32 * (2 * p + q)
            both = jnp.where(from_left(32), fp[0, n:n + 32], fp[1, n:n + 32])
            for c in range(32):
                r = box_row(2 * (c // 8) + p) + 32 * (c % 8)
                a[p, q, 3, r:r + 32] = pltpu.roll(both, (126 - 4 * c) % 128, 1)

    def edges(n):
        lane = lanes(n)
        return lane == 0, lane == 127

    def weigh(r, n):
        first, last = edges(n)
        here = [pe[k, pl.ds(r, n)] for k in range(4)]
        fxs = []
        for k in range(4):
            f = harmonic(here[k], pe[k, pl.ds(r + 1, n)])
            fx[k, pl.ds(r, n)] = f
            fxs.append(f)
        ahead = [pltpu.roll(x, 127, 1) for x in here]
        fys = [harmonic(here[k], jnp.where(last, ahead[(k + 1) % 4], ahead[k])) for k in range(4)]
        behind = [pltpu.roll(x, 1, 1) for x in fys]
        for k in range(4):
            west = fx[k, pl.ds(r - 1, n)]
            south = jnp.where(first, behind[(k + 3) % 4], behind[k])
            total = fxs[k] + west + fys[k] + south
            inv = 2.0 * recip(jnp.maximum(total, TINY))
            w[0, k, pl.ds(r, n)] = fxs[k] * inv
            w[1, k, pl.ds(r, n)] = west * inv
            w[2, k, pl.ds(r, n)] = fys[k] * inv
            w[3, k, pl.ds(r, n)] = south * inv

    def weigh_step(g, carry):
        weigh(pl.multiple_of(24 + WEIGH_ROWS * g, 8), WEIGH_ROWS)
        return carry

    weigh(8, 16)
    lax.fori_loop(0, 1152 // WEIGH_ROWS, weigh_step, 0)
    for c in copies[early:]:
        c.wait()

    def smooth(src, p, q, off, n, ws, blocks):
        first, last = edges(n)
        pairs = ((0, 1), (2, 3)) if q == 0 else ((3, 0), (1, 2))
        got = {}
        for x, y in pairs:
            bx, by = src[p, q, x, pl.ds(off, n)], src[p, q, y, pl.ds(off, n)]
            rx, ry = pltpu.roll(bx, 1, 1), pltpu.roll(by, 1, 1)
            lx, ly = pltpu.roll(bx, 127, 1), pltpu.roll(by, 127, 1)
            near = {
                x: (bx, jnp.where(last, ly, lx), jnp.where(first, 0.0, rx)),
                y: (by, jnp.where(last, 0.0, ly), jnp.where(first, rx, ry)),
            }
            for k in (x, y):
                if k not in blocks:
                    continue
                c, north, south = near[k]
                we, ww, wn, wsouth = ws[k]
                s = c + wn * north + wsouth * south
                s = s + we * src[p, q, k, pl.ds(off + 1, n)] + ww * src[p, q, k, pl.ds(off - 1, n)]
                got[k] = jnp.where(c > 0, s, 0.0)
        return got

    def group(src, wrow, offs, n, blocks):
        ws = {k: [w[d, k, pl.ds(wrow, n)] for d in range(4)] for k in blocks}
        s = {(p, q): smooth(src, p, q, offs[p], n, ws, blocks) for p in (0, 1) for q in (0, 1)}
        done = {}
        for k in blocks:
            total = (s[0, 0][k] + s[0, 1][k]) + (s[1, 0][k] + s[1, 1][k])
            inv = recip(jnp.maximum(total, TINY))
            for p in (0, 1):
                for q in (0, 1):
                    done[p, q, k] = s[p, q][k] * inv
        return done

    def first_pass(wrow, offs, n):
        for (p, q, k), v in group(a, wrow, offs, n, (0, 1, 2, 3)).items():
            b[p, q, k, pl.ds(offs[p], n)] = v

    first_pass(8, (8, 8), 8)
    first_pass(1168, (1208, 1208), 8)
    for k in range(9):
        even, odd = chunk_rows(k)

        def step(g, carry, k=k, even=even, odd=odd):
            r = pl.multiple_of(FIRST_ROWS * g, 8)
            offs = (pl.multiple_of(even + r, 8), pl.multiple_of(odd + r, 8))
            for u in range(0, FIRST_ROWS, SUB):
                first_pass(pl.multiple_of(16 + 128 * k + r + u, 8), tuple(pl.multiple_of(o + u, 8) for o in offs), SUB)
            return carry

        lax.fori_loop(0, 128 // FIRST_ROWS, step, 0)

    stores = []
    for k in range(9):
        even, odd = chunk_rows(k)
        boxes = ((k // 2) * 2, ((k + 1) // 2) * 2 - 1)

        def step(g, carry, k=k, even=even, odd=odd, boxes=boxes):
            r = pl.multiple_of(SECOND_ROWS * g, 8)
            offs = (pl.multiple_of(even + r, 8), pl.multiple_of(odd + r, 8))
            for u in range(0, SECOND_ROWS, SUB):
                done = group(b, pl.multiple_of(16 + 128 * k + r + u, 8), tuple(pl.multiple_of(o + u, 8) for o in offs), SUB, (0, 1, 2))
                for p in (0, 1):
                    i = boxes[p]
                    if not 0 <= i < 8:
                        continue
                    for j in (0, 1):
                        for h in (0, 1):
                            res[i, j, h, pl.ds(128 * (k - i) + r + u, SUB)] = done[p, j, j + h]
            return carry

        lax.fori_loop(0, 128 // SECOND_ROWS, step, 0)
        if k >= 1:
            for j in (0, 1):
                for h in (0, 1):
                    c = pltpu.make_async_copy(res.at[k - 1, j, h], out.at[k - 1, j, :, pl.ds(128 * h, 128)], sem_out.at[len(stores)])
                    c.start()
                    stores.append(c)
    for c in stores:
        c.wait()


def both_ways(pairs):
    return pairs + [(d, s) for s, d in pairs]


def swap(block, axis, parity):
    n = lax.axis_size(axis)
    return lax.ppermute(block, axis, both_ways([(i, i + 1) for i in range(parity, n - 1, 2)]))


def hbm(n):
    return [pl.BlockSpec(memory_space=pltpu.HBM)] * n


def vmem(n):
    return [pl.BlockSpec(memory_space=pltpu.VMEM)] * n


def bundle(rows):
    return jax.ShapeDtypeStruct((rows, 128), F32)


def local(permeability, basis, support):
    params = pltpu.CompilerParams(vmem_limit_bytes=VMEM_LIMIT)
    dma = pltpu.SemaphoreType.DMA
    sx_e, sx_o = pl.pallas_call(
        pack_x_kernel,
        out_shape=[bundle(XR), bundle(XR)],
        in_specs=hbm(2),
        out_specs=vmem(2),
        scratch_shapes=[
            pltpu.VMEM((2, 2, 72, 128), F32),
            pltpu.VMEM((2, 2, 144, 128), F32),
            pltpu.VMEM((2, 24, 128), F32),
            dma((22,)),
            dma((12,)),
        ],
        compiler_params=pltpu.CompilerParams(vmem_limit_bytes=PACK_LIMIT),
        name="pack_x",
    )(permeability, basis)
    rx_o = swap(sx_o, "gx", 1)
    rx_e = swap(sx_e, "gx", 0)
    sy_e, sy_o = pl.pallas_call(
        pack_y_kernel,
        out_shape=[bundle(YR), bundle(YR)],
        in_specs=hbm(3),
        out_specs=vmem(2),
        scratch_shapes=[
            pltpu.VMEM((2, 1024, 128), F32),
            pltpu.VMEM((2, 8, 256, 128), F32),
            pltpu.VMEM((160, 128), F32),
            pltpu.VMEM((2, 512, 128), F32),
            dma((22,)),
            dma((4,)),
        ],
        compiler_params=pltpu.CompilerParams(vmem_limit_bytes=PACK_LIMIT),
        name="pack_y",
    )(permeability, basis, sx_e)
    sy_e, sy_o = pl.pallas_call(
        gate_kernel,
        out_shape=[bundle(YR), bundle(YR)],
        in_specs=hbm(3),
        out_specs=hbm(2),
        input_output_aliases={0: 0, 1: 1},
        compiler_params=pltpu.CompilerParams(vmem_limit_bytes=1024 * 1024),
        name="gate",
    )(sy_e, sy_o, rx_e)
    ry_o = swap(sy_o, "gy", 1)
    ry_e = swap(sy_e, "gy", 0)
    sc_e, sc_o = pl.pallas_call(
        corner_kernel,
        out_shape=[bundle(CR), bundle(CR)],
        in_specs=vmem(2),
        out_specs=vmem(2),
        compiler_params=pltpu.CompilerParams(vmem_limit_bytes=4 * 1024 * 1024),
        name="corner",
    )(rx_e, rx_o)
    rc_o = swap(sc_o, "gy", 1)
    rc_e = swap(sc_e, "gy", 0)
    return pl.pallas_call(
        main_kernel,
        out_shape=jax.ShapeDtypeStruct(basis.shape, F32),
        in_specs=hbm(8),
        out_specs=pl.BlockSpec(memory_space=pltpu.HBM),
        scratch_shapes=[
            pltpu.VMEM((2, 2, 4, ROWS, 128), F32),
            pltpu.VMEM((2, 2, 4, ROWS, 128), F32),
            pltpu.VMEM((4, PROWS, 128), F32),
            pltpu.VMEM((4, PROWS, 128), F32),
            pltpu.VMEM((4, 4, PROWS, 128), F32),
            pltpu.VMEM((2, 1024, 128), F32),
            pltpu.VMEM((2, 512, 128), F32),
            pltpu.VMEM((2, 160, 128), F32),
            pltpu.VMEM((2, 144, 128), F32),
            pltpu.VMEM((2, 2, 24, 128), F32),
            pltpu.VMEM((2, 2, 72, 128), F32),
            pltpu.VMEM((8, 2, 2, 256, 128), F32),
            dma((96,)),
            dma((32,)),
        ],
        compiler_params=params,
        name="smooth",
    )(permeability, basis, rx_e, rx_o, ry_e, ry_o, rc_e, rc_o)


def solution(mesh):
    placed = (P("gx", "gy"), P("gx", "gy", None, None), P("gx", "gy", None, None))
    return jax.shard_map(
        local, mesh=mesh, in_specs=placed, out_specs=P("gx", "gy", None, None), check_vma=False
    )
```

```python
import jax
import jax.numpy as jnp
from jax import lax
from jax.experimental import pallas as pl
from jax.experimental.pallas import tpu as pltpu
from jax.sharding import PartitionSpec as P


F32 = jnp.float32
TINY = 1.1754944e-38
ROWS = 1224
PROWS = 1184
XR = 744
YR = 2720
CR = 480
GUARDS = ((0, 16, 280, 544, 808, 1072, 1216), (0, 144, 408, 672, 936, 1200, 1216))
VMEM_LIMIT = 60 * 1024 * 1024
SUB = 8
PACK_LIMIT = 16 * 1024 * 1024
WEIGH_ROWS = 128
FIRST_ROWS = 128
SECOND_ROWS = 128


def box_row(i):
    return 24 + 264 * (i // 2) if i % 2 == 0 else 152 + 264 * ((i - 1) // 2)


def chunk_rows(k):
    even = 24 + 264 * (k // 2) + 128 * (k % 2)
    odd = 152 + 264 * ((k - 1) // 2) + 128 * ((k - 1) % 2)
    return even, odd


def lanes(rows):
    return lax.broadcasted_iota(jnp.int32, (rows, 128), 1)


def sides():
    sx = 1 - lax.rem(lax.axis_index("gx"), 2)
    sy = 1 - lax.rem(lax.axis_index("gy"), 2)
    return (sx, 1 - sx), (sy, 1 - sy)


def pack_windows(pieces, first):
    rows = pieces[0].shape[0]
    lane = lanes(rows)
    out = jnp.zeros((rows, 128), F32)
    for c, piece in enumerate(pieces):
        turned = pltpu.roll(piece, (4 * c - first) % 128, 1)
        out = jnp.where(lane // 4 == c, turned, out)
    return out


def joined(pv, r, n):
    return jnp.where(lanes(n) < 64, pv[1, r:r + n], pv[0, r:r + n])


def mover(sem):
    moves = []

    def move(src, dst):
        c = pltpu.make_async_copy(src, dst, sem.at[len(moves)])
        c.start()
        moves.append(c)

    return moves, move


def pack_x_kernel(perm, basis, sx_e, sx_o, pv, mid, xfringe, sem, sem_in):
    (xe, xo), _ = sides()
    loads, load = mover(sem_in)
    moves, move = mover(sem)
    for t in (0, 1):
        for h in (0, 1):
            load(perm.at[pl.ds(952 * t, 72), pl.ds(128 * h, 128)], pv.at[t, h])
        for q in (0, 1):
            load(basis.at[7 * t, q, pl.ds(120 * t, 136), pl.ds(128 * (1 - q), 128)], mid.at[t, q, pl.ds(0, 136)])
            load(basis.at[1 + 5 * t, q, pl.ds(248 * t, 8), pl.ds(128 * (1 - q), 128)], mid.at[t, q, pl.ds(136, 8)])
    for t, out in ((xo, sx_o), (xe, sx_e)):
        for j in (0, 1):
            for h in (0, 1):
                at = 144 * (2 * j + h)
                r0 = pl.multiple_of(120 * t, 8)
                r1 = pl.multiple_of(248 * t, 8)
                move(basis.at[7 * t, j, pl.ds(r0, 136), pl.ds(128 * h, 128)], out.at[pl.ds(at, 136)])
                move(basis.at[1 + 5 * t, j, pl.ds(r1, 8), pl.ds(128 * h, 128)], out.at[pl.ds(at + 136, 8)])
        for h in (0, 1):
            r2 = pl.multiple_of(952 * t, 8)
            move(perm.at[pl.ds(r2, 72), pl.ds(128 * h, 128)], out.at[pl.ds(576 + 72 * h, 72)])
    for c in loads:
        c.wait()
    for t in (0, 1):
        for q in (0, 1):
            pieces = [mid[t, q, 8 * c:8 * c + 8] for c in range(18)]
            xfringe[t, 8 * q:8 * q + 8] = pack_windows(pieces, 126)
        xfringe[t, 16:24] = pack_windows([joined(pv[t], 8 * c, 8) for c in range(9)], 62)
    for t, out in ((xo, sx_o), (xe, sx_e)):
        move(xfringe.at[t], out.at[pl.ds(720, 24)])
    for c in moves:
        c.wait()


def pack_y_kernel(perm, basis, after, sy_e, sy_o, pv, mid, fringe, strip, sem, sem_in):
    _, (ye, yo) = sides()
    loads, load = mover(sem_in)
    moves, move = mover(sem)
    for h in (0, 1):
        load(perm.at[:, pl.ds(128 * h, 128)], pv.at[h])
    for q in (0, 1):
        load(basis.at[:, q, :, pl.ds(128 * (1 - q), 128)], mid.at[q])
    for s, out in ((yo, sy_o), (ye, sy_e)):
        lane = pl.multiple_of(s * 128, 128)
        for i in range(8):
            move(basis.at[i, s, :, pl.ds(lane, 128)], out.at[pl.ds(256 * i, 256)])
    for c in loads:
        c.wait()
    lane = lanes(32)
    for p in (0, 1):
        for q in (0, 1):
            pieces = [mid[q, 2 * (c // 8) + p, 32 * (c % 8):32 * (c % 8) + 32] for c in range(32)]
            fringe[32 * (2 * p + q):32 * (2 * p + q) + 32] = pack_windows(pieces, 126)
    fringe[128:160] = pack_windows([joined(pv, 32 * c, 32) for c in range(32)], 62)
    for h in (0, 1):
        for r in range(0, 512, 32):
            low = pv[h, r:r + 32]
            high = pltpu.roll(pv[h, r + 512:r + 544], 64, 1)
            keep = lane >= 64 if h else lane < 64
            strip[h, r:r + 32] = jnp.where(keep, low, high)
    for s, out in ((yo, sy_o), (ye, sy_e)):
        move(fringe.at[pl.ds(0, 128)], out.at[pl.ds(2048, 128)])
        move(strip.at[s], out.at[pl.ds(2176, 512)])
        move(fringe.at[pl.ds(128, 32)], out.at[pl.ds(2688, 32)])
    for c in moves:
        c.wait()


def gate_kernel(y_e, y_o, after, out_e, out_o):
    pass


def corner_kernel(rx_e, rx_o, sc_e, sc_o):
    _, (ye, yo) = sides()
    for s, out in ((yo, sc_o), (ye, sc_e)):
        for slot, rx in ((0, rx_e), (1, rx_o)):
            base = 240 * slot
            m = pl.multiple_of(432 * s, 8)
            k = pl.multiple_of(576 + 72 * s, 8)
            out[base:base + 144] = rx[pl.ds(m, 144)]
            out[base + 144:base + 168] = rx[720:744]
            out[base + 168:base + 240] = rx[pl.ds(k, 72)]


def recip(x):
    r = pl.reciprocal(x, approx=True)
    return r * (2.0 - x * r)


def harmonic(a, b):
    return 2.0 * a * b * recip(jnp.maximum(a + b, TINY))


def main_kernel(perm, basis, rx_e, rx_o, ry_e, ry_o, rc_e, rc_o, out,
                a, b, pe, fx, w, pv, ps, fp, xp, cf, cp, res, sem, sem_out):
    (xe, xo), (ye, yo) = sides()
    copies = []

    def load(src, dst):
        c = pltpu.make_async_copy(src, dst, sem.at[len(copies)])
        c.start()
        copies.append(c)

    for h in (0, 1):
        load(perm.at[:, pl.ds(128 * h, 128)], pv.at[h])
    for s, ry in ((ye, ry_e), (yo, ry_o)):
        load(ry.at[pl.ds(2176, 512)], ps.at[s])
        load(ry.at[pl.ds(2048, 128)], fp.at[s, pl.ds(0, 128)])
        load(ry.at[pl.ds(2688, 32)], fp.at[s, pl.ds(128, 32)])
    for t, rx in ((xe, rx_e), (xo, rx_o)):
        load(rx.at[pl.ds(576, 144)], xp.at[t])
    for s, rc in ((ye, rc_e), (yo, rc_o)):
        for slot, t in ((0, xe), (1, xo)):
            load(rc.at[pl.ds(240 * slot + 144, 24)], cf.at[s, t])
            load(rc.at[pl.ds(240 * slot + 168, 72)], cp.at[s, t])
    early = len(copies)
    for i in range(8):
        for j in (0, 1):
            for h in (0, 1):
                load(basis.at[i, j, :, pl.ds(128 * h, 128)], a.at[i % 2, j, j + h, pl.ds(box_row(i), 256)])
        for s, ry in ((ye, ry_e), (yo, ry_o)):
            load(ry.at[pl.ds(256 * i, 256)], a.at[i % 2, 1 - s, 2 * s, pl.ds(box_row(i), 256)])

    def place(src, at, t, q, blk):
        r0 = pl.multiple_of(8 + 1072 * t, 8)
        r1 = pl.multiple_of(8 + 1200 * t, 8)
        load(src.at[pl.ds(at, 136)], a.at[1 - t, q, blk, pl.ds(r0, 136)])
        load(src.at[pl.ds(at + 136, 8)], a.at[t, q, blk, pl.ds(r1, 8)])

    for t, rx in ((xe, rx_e), (xo, rx_o)):
        for j in (0, 1):
            for h in (0, 1):
                place(rx, 144 * (2 * j + h), t, j, j + h)
    for s, rc in ((ye, rc_e), (yo, rc_o)):
        for slot, t in ((0, xe), (1, xo)):
            place(rc, 240 * slot, t, 1 - s, 2 * s)

    zero = jnp.zeros((8, 128), F32)
    for p in (0, 1):
        for q in (0, 1):
            for k in range(4):
                for g in GUARDS[p]:
                    a[p, q, k, g:g + 8] = zero
                    b[p, q, k, g:g + 8] = zero
    for k in range(4):
        pe[k, 0:8] = zero
        pe[k, PROWS - 8:PROWS] = zero
        fx[k, 0:8] = zero

    for c in copies[:early]:
        c.wait()

    def from_left(n):
        return lanes(n) % 4 < 2

    half32, half8 = lanes(32) < 64, lanes(8) < 64

    def fill(at, n, half, left, own0, own1, right):
        u0 = pltpu.roll(own0, 64, 1)
        u1 = pltpu.roll(own1, 64, 1)
        pe[0, at:at + n] = jnp.where(half, left, u0)
        pe[1, at:at + n] = jnp.where(half, u0, u1)
        pe[2, at:at + n] = jnp.where(half, u1, right)

    for r in range(0, 1024, 32):
        left, right = ps[0, r % 512:r % 512 + 32], ps[1, r % 512:r % 512 + 32]
        if r < 512:
            left, right = pltpu.roll(left, 64, 1), pltpu.roll(right, 64, 1)
        fill(80 + r, 32, half32, left, pv[0, r:r + 32], pv[1, r:r + 32], right)
    for t in (0, 1):
        for c in range(9):
            r = 8 * c
            left, right = pltpu.roll(cp[0, t, r:r + 8], 64, 1), pltpu.roll(cp[1, t, r:r + 8], 64, 1)
            fill(8 + 1096 * t + r, 8, half8, left, xp[t, r:r + 8], xp[t, 72 + r:80 + r], right)
        both = jnp.where(from_left(8), cf[0, t, 16:24], cf[1, t, 16:24])
        for c in range(9):
            r = 8 + 1096 * t + 8 * c
            pe[3, r:r + 8] = pltpu.roll(both, (126 - 4 * c) % 128, 1)
        for q in (0, 1):
            both = jnp.where(from_left(8), cf[0, t, 8 * q:8 * q + 8], cf[1, t, 8 * q:8 * q + 8])
            for c in range(18):
                r = 8 + 1072 * t + 8 * c if c < 17 else 8 + 1200 * t
                a[1 - t if c < 17 else t, q, 3, r:r + 8] = pltpu.roll(both, (126 - 4 * c) % 128, 1)
    both = jnp.where(from_left(32), fp[0, 128:160], fp[1, 128:160])
    for c in range(32):
        pe[3, 80 + 32 * c:112 + 32 * c] = pltpu.roll(both, (126 - 4 * c) % 128, 1)
    for p in (0, 1):
        for q in (0, 1):
            n = 32 * (2 * p + q)
            both = jnp.where(from_left(32), fp[0, n:n + 32], fp[1, n:n + 32])
            for c in range(32):
                r = box_row(2 * (c // 8) + p) + 32 * (c % 8)
                a[p, q, 3, r:r + 32] = pltpu.roll(both, (126 - 4 * c) % 128, 1)

    def edges(n):
        lane = lanes(n)
        return lane == 0, lane == 127

    def weigh(r, n):
        first, last = edges(n)
        here = [pe[k, pl.ds(r, n)] for k in range(4)]
        fxs = []
        for k in range(4):
            f = harmonic(here[k], pe[k, pl.ds(r + 1, n)])
            fx[k, pl.ds(r, n)] = f
            fxs.append(f)
        ahead = [pltpu.roll(x, 127, 1) for x in here]
        fys = [harmonic(here[k], jnp.where(last, ahead[(k + 1) % 4], ahead[k])) for k in range(4)]
        behind = [pltpu.roll(x, 1, 1) for x in fys]
        for k in range(4):
            west = fx[k, pl.ds(r - 1, n)]
            south = jnp.where(first, behind[(k + 3) % 4], behind[k])
            total = fxs[k] + west + fys[k] + south
            inv = 2.0 * recip(jnp.maximum(total, TINY))
            w[0, k, pl.ds(r, n)] = fxs[k] * inv
            w[1, k, pl.ds(r, n)] = west * inv
            w[2, k, pl.ds(r, n)] = fys[k] * inv
            w[3, k, pl.ds(r, n)] = south * inv

    def weigh_step(g, carry):
        weigh(pl.multiple_of(24 + WEIGH_ROWS * g, 8), WEIGH_ROWS)
        return carry

    weigh(8, 16)
    lax.fori_loop(0, 1152 // WEIGH_ROWS, weigh_step, 0)
    for c in copies[early:]:
        c.wait()

    def smooth(src, p, q, off, n, ws, blocks):
        first, last = edges(n)
        pairs = ((0, 1), (2, 3)) if q == 0 else ((3, 0), (1, 2))
        got = {}
        for x, y in pairs:
            bx, by = src[p, q, x, pl.ds(off, n)], src[p, q, y, pl.ds(off, n)]
            rx, ry = pltpu.roll(bx, 1, 1), pltpu.roll(by, 1, 1)
            lx, ly = pltpu.roll(bx, 127, 1), pltpu.roll(by, 127, 1)
            near = {
                x: (bx, jnp.where(last, ly, lx), jnp.where(first, 0.0, rx)),
                y: (by, jnp.where(last, 0.0, ly), jnp.where(first, rx, ry)),
            }
            for k in (x, y):
                if k not in blocks:
                    continue
                c, north, south = near[k]
                we, ww, wn, wsouth = ws[k]
                s = c + wn * north + wsouth * south
                s = s + we * src[p, q, k, pl.ds(off + 1, n)] + ww * src[p, q, k, pl.ds(off - 1, n)]
                got[k] = jnp.where(c > 0, s, 0.0)
        return got

    def group(src, wrow, offs, n, blocks):
        ws = {k: [w[d, k, pl.ds(wrow, n)] for d in range(4)] for k in blocks}
        s = {(p, q): smooth(src, p, q, offs[p], n, ws, blocks) for p in (0, 1) for q in (0, 1)}
        done = {}
        for k in blocks:
            total = (s[0, 0][k] + s[0, 1][k]) + (s[1, 0][k] + s[1, 1][k])
            inv = recip(jnp.maximum(total, TINY))
            for p in (0, 1):
                for q in (0, 1):
                    done[p, q, k] = s[p, q][k] * inv
        return done

    def first_pass(wrow, offs, n):
        for (p, q, k), v in group(a, wrow, offs, n, (0, 1, 2, 3)).items():
            b[p, q, k, pl.ds(offs[p], n)] = v

    first_pass(8, (8, 8), 8)
    first_pass(1168, (1208, 1208), 8)
    for k in range(9):
        even, odd = chunk_rows(k)

        def step(g, carry, k=k, even=even, odd=odd):
            r = pl.multiple_of(FIRST_ROWS * g, 8)
            offs = (pl.multiple_of(even + r, 8), pl.multiple_of(odd + r, 8))
            for u in range(0, FIRST_ROWS, SUB):
                first_pass(pl.multiple_of(16 + 128 * k + r + u, 8), tuple(pl.multiple_of(o + u, 8) for o in offs), SUB)
            return carry

        lax.fori_loop(0, 128 // FIRST_ROWS, step, 0)

    stores = []
    for k in range(9):
        even, odd = chunk_rows(k)
        boxes = ((k // 2) * 2, ((k + 1) // 2) * 2 - 1)

        def step(g, carry, k=k, even=even, odd=odd, boxes=boxes):
            r = pl.multiple_of(SECOND_ROWS * g, 8)
            offs = (pl.multiple_of(even + r, 8), pl.multiple_of(odd + r, 8))
            for u in range(0, SECOND_ROWS, SUB):
                done = group(b, pl.multiple_of(16 + 128 * k + r + u, 8), tuple(pl.multiple_of(o + u, 8) for o in offs), SUB, (0, 1, 2))
                for p in (0, 1):
                    i = boxes[p]
                    if not 0 <= i < 8:
                        continue
                    for j in (0, 1):
                        for h in (0, 1):
                            res[i, j, h, pl.ds(128 * (k - i) + r + u, SUB)] = done[p, j, j + h]
            return carry

        lax.fori_loop(0, 128 // SECOND_ROWS, step, 0)
        if k >= 1:
            for j in (0, 1):
                for h in (0, 1):
                    c = pltpu.make_async_copy(res.at[k - 1, j, h], out.at[k - 1, j, :, pl.ds(128 * h, 128)], sem_out.at[len(stores)])
                    c.start()
                    stores.append(c)
    for c in stores:
        c.wait()


def both_ways(pairs):
    return pairs + [(d, s) for s, d in pairs]


def swap(block, axis, parity):
    n = lax.axis_size(axis)
    return lax.ppermute(block, axis, both_ways([(i, i + 1) for i in range(parity, n - 1, 2)]))


def hbm(n):
    return [pl.BlockSpec(memory_space=pltpu.HBM)] * n


def vmem(n):
    return [pl.BlockSpec(memory_space=pltpu.VMEM)] * n


def bundle(rows):
    return jax.ShapeDtypeStruct((rows, 128), F32)


def local(permeability, basis, support):
    params = pltpu.CompilerParams(vmem_limit_bytes=VMEM_LIMIT)
    dma = pltpu.SemaphoreType.DMA
    sx_e, sx_o = pl.pallas_call(
        pack_x_kernel,
        out_shape=[bundle(XR), bundle(XR)],
        in_specs=hbm(2),
        out_specs=vmem(2),
        scratch_shapes=[
            pltpu.VMEM((2, 2, 72, 128), F32),
            pltpu.VMEM((2, 2, 144, 128), F32),
            pltpu.VMEM((2, 24, 128), F32),
            dma((22,)),
            dma((12,)),
        ],
        compiler_params=pltpu.CompilerParams(vmem_limit_bytes=PACK_LIMIT),
        name="pack_x",
    )(permeability, basis)
    rx_o = swap(sx_o, "gx", 1)
    rx_e = swap(sx_e, "gx", 0)
    sy_e, sy_o = pl.pallas_call(
        pack_y_kernel,
        out_shape=[bundle(YR), bundle(YR)],
        in_specs=hbm(3),
        out_specs=vmem(2),
        scratch_shapes=[
            pltpu.VMEM((2, 1024, 128), F32),
            pltpu.VMEM((2, 8, 256, 128), F32),
            pltpu.VMEM((160, 128), F32),
            pltpu.VMEM((2, 512, 128), F32),
            dma((22,)),
            dma((4,)),
        ],
        compiler_params=pltpu.CompilerParams(vmem_limit_bytes=PACK_LIMIT),
        name="pack_y",
    )(permeability, basis, sx_e)
    sy_e, sy_o = pl.pallas_call(
        gate_kernel,
        out_shape=[bundle(YR), bundle(YR)],
        in_specs=hbm(3),
        out_specs=hbm(2),
        input_output_aliases={0: 0, 1: 1},
        compiler_params=pltpu.CompilerParams(vmem_limit_bytes=1024 * 1024),
        name="gate",
    )(sy_e, sy_o, rx_e)
    ry_o = swap(sy_o, "gy", 1)
    ry_e = swap(sy_e, "gy", 0)
    sc_e, sc_o = pl.pallas_call(
        corner_kernel,
        out_shape=[bundle(CR), bundle(CR)],
        in_specs=vmem(2),
        out_specs=vmem(2),
        compiler_params=pltpu.CompilerParams(vmem_limit_bytes=4 * 1024 * 1024),
        name="corner",
    )(rx_e, rx_o)
    rc_o = swap(sc_o, "gy", 1)
    rc_e = swap(sc_e, "gy", 0)
    return pl.pallas_call(
        main_kernel,
        out_shape=jax.ShapeDtypeStruct(basis.shape, F32),
        in_specs=hbm(8),
        out_specs=pl.BlockSpec(memory_space=pltpu.HBM),
        scratch_shapes=[
            pltpu.VMEM((2, 2, 4, ROWS, 128), F32),
            pltpu.VMEM((2, 2, 4, ROWS, 128), F32),
            pltpu.VMEM((4, PROWS, 128), F32),
            pltpu.VMEM((4, PROWS, 128), F32),
            pltpu.VMEM((4, 4, PROWS, 128), F32),
            pltpu.VMEM((2, 1024, 128), F32),
            pltpu.VMEM((2, 512, 128), F32),
            pltpu.VMEM((2, 160, 128), F32),
            pltpu.VMEM((2, 144, 128), F32),
            pltpu.VMEM((2, 2, 24, 128), F32),
            pltpu.VMEM((2, 2, 72, 128), F32),
            pltpu.VMEM((8, 2, 2, 256, 128), F32),
            dma((96,)),
            dma((32,)),
        ],
        compiler_params=params,
        name="smooth",
    )(permeability, basis, rx_e, rx_o, ry_e, ry_o, rc_e, rc_o)


def solution(mesh):
    placed = (P("gx", "gy"), P("gx", "gy", None, None), P("gx", "gy", None, None))
    return jax.shard_map(
        local, mesh=mesh, in_specs=placed, out_specs=P("gx", "gy", None, None), check_vma=False
    )
```
